32 devices in a mesh: sky: 2 (over y), band: 4 (over z), lon: 2 (over x), pol: 2 (over core).
Axes of the slice: x: 2, y: 2, z: 4, core: 2. Of those that a mesh axis runs over, the one named last changes fastest.
Arguments:
- residual_cot: float32 [2, 4, 128, 256], P('pol', 'sky', 'band', 'lon'), parts along dimension 1, may hold values from -6 to 6
- splat_weights: float32 [8, 128, 256], P('sky', 'band', 'lon'), parts along dimension 0, may hold values from 0 to 1
- sample_cycle: int32 [256, 256], P(('sky', 'band'), 'lon'), parts along dimension 0, may hold values from 0 to 1
- sample_pixel: int32 [256, 256], P(('sky', 'band'), 'lon'), parts along dimension 0, may hold values from 0 to 6398
- live_rows: int32 [16], P(('sky', 'band', 'lon')), parts along dimension 0, may hold values from 1 to 32, 128 in all
- table_w: bfloat16 [1536, 4, 3073], P(('band', 'lon', 'pol')), may hold values from -3 to 3
- table_x: bfloat16 [1536, 4, 3073], P(('band', 'lon', 'pol')), may hold values from -3 to 3
- filters: float32 [2, 3072], replicated, may hold values from 0.5 to 2
Outputs:
- gradient: bfloat16 [1536, 4, 2, 3073], P(('band', 'lon', 'pol'), 'sky'), parts along dimension 1
The draws below stay inside these ranges and needn't reach their ends.
There are 2 independent parts, one for each index of `sky`. The reference program is written for one: setup_inputs(seed, part) draws one part's arguments, and reference() takes and returns one part's arrays. A program takes and returns all parts, laid end to end along the dimension named above; an argument that names none is the same for every part. Nothing has to cross between parts.
Inputs may be any that keep to these rules, and one draw needn't show every extreme that they name: `live_rows`: some block has exactly 32 live rows.
All inputs are finite; a program needn't handle non-finite values.
Results may differ from the reference program's by a relative error of at most 0.0059.
Values may be sent and summed in bfloat16 or wider, within the bound.
No kernel may reach another device: no remote copies, remote signals or barrier semaphores. Data moves between devices by JAX's collectives and lax.ppermute only.
A program may use at most 128 MiB of HBM per device.

```python
import math
import jax
import jax.numpy as jnp
import numpy as np
from jax import lax

NSIM = 2
ROWS_DEV = 32
BAND_CYCLES = 1
NPHI = 12288
M = 3072
RIM = 128
NRING = 4
PIX_DEV = 6144
PAIRS = 1536
N_BAND = 4
N_LON = 2


def set_ends(drawn, stream_key, least, top_value):
    longest = drawn.shape.index(max(drawn.shape))
    spots = []
    for shift in (0, 1):
        where = [jax.random.randint(jax.random.fold_in(stream_key, axis), (), 0, length) for axis, length in enumerate(drawn.shape)]
        where[longest] = (where[longest] + shift) % drawn.shape[longest]
        spots.append(tuple(where))
    return drawn.at[spots[0]].set(least).at[spots[1]].set(top_value)


def steps_of(own_key, dims, pieces, low, largest):
    def one(position, parts):
        heights = jax.random.uniform(jax.random.fold_in(jax.random.fold_in(own_key, 6), position), (parts,), jnp.float32, low / len(pieces), largest / len(pieces))
        return jnp.repeat(jnp.exp(heights), dims[position] // parts).reshape((-1,) + (1,) * (len(dims) - position - 1))

    factor_of = one(*pieces[0])
    for cut in pieces[1:]:
        factor_of = factor_of * one(*cut)
    return factor_of


def split_up(count, total, limit, lean):
    portions = [(1 << 20) // math.isqrt(grade ** lean) + 1 for grade in range(2, count + 1)]
    surplus, given = total - limit - (count - 1), [1] * (count - 1)
    while surplus > 0:
        free = [i for i in range(count - 1) if given[i] < limit]
        pool, budget = sum([portions[i] for i in free]), surplus
        for i in free:
            extra = min(limit - given[i], max(1, budget * portions[i] // pool), surplus)
            given[i] = given[i] + extra
            surplus = surplus - extra
    return np.array([limit] + given)


def uneven(key, count, total, reach, skew):
    if count == 2:
        one = jax.random.randint(key, (), max(1, total - reach), min(reach, total - 1) + 1)
        return jnp.stack([one, total - one])
    lengths = jnp.asarray(split_up(count, total, reach, skew), jnp.int32)
    pairs = (count - 1) // 2
    giver, taker = lengths[1:1 + 2 * pairs:2], lengths[2:2 + 2 * pairs:2]
    margin = jnp.minimum(giver - 1, reach - taker)
    passed = jax.random.randint(jax.random.fold_in(key, 1), (pairs,), 0, 1 << 20) % (margin + 1)
    lengths = lengths.at[1:1 + 2 * pairs:2].set(giver - passed).at[2:2 + 2 * pairs:2].set(taker + passed)
    return lengths[jax.random.permutation(jax.random.fold_in(key, 2), count)]


def gaussian(key, shape, deviation, reach, split=(), held_as=jnp.bfloat16):
    drawn = deviation * jax.random.normal(key, shape, jnp.float32)
    if split:
        drawn = drawn * steps_of(key, shape, split, -0.22, 0.18)
    return jnp.clip(drawn, -reach, reach).astype(held_as)


def setup_inputs(seed: int = 0, part: int = 0) -> dict:
    arg_keys = jax.random.split(jax.random.key(seed), 9)
    own_keys = jax.random.split(jax.random.fold_in(arg_keys[8], part), 9)
    residual_cot = gaussian(own_keys[0], (2, NSIM, N_BAND * ROWS_DEV, N_LON * 128), 1.0, 6.0, ((0, 2), (2, 4), (3, 2)), jnp.float32)
    splat_weights = jnp.clip(1.0 * jax.random.uniform(own_keys[1], (4, N_BAND * ROWS_DEV, N_LON * 128), jnp.float32) ** steps_of(own_keys[1], (4, N_BAND * ROWS_DEV, N_LON * 128), ((1, 4), (2, 2)), -0.2, 0.2), 0.0, 1.0)
    sample_cycle = set_ends(jax.random.randint(own_keys[2], (N_BAND * ROWS_DEV, N_LON * 128), 0, BAND_CYCLES + 1), jax.random.fold_in(own_keys[2], 1), 0, BAND_CYCLES).astype(jnp.int32)
    sample_pixel = set_ends(jax.random.randint(own_keys[3], (N_BAND * ROWS_DEV, N_LON * 128), 0, PIX_DEV + 2 * RIM - 1), jax.random.fold_in(own_keys[3], 1), 0, (PIX_DEV + 2 * RIM - 1) - 1).astype(jnp.int32)
    live_rows = uneven(own_keys[4], N_BAND * N_LON, N_BAND * N_LON * ROWS_DEV // 2, ROWS_DEV, 2).astype(jnp.int32)
    table_w = gaussian(arg_keys[5], (PAIRS, NRING, M + 1), NRING ** -0.5, 3.0, ((0, 16),))
    table_x = gaussian(arg_keys[6], (PAIRS, NRING, M + 1), NRING ** -0.5, 3.0, ((0, 16),))
    filters = jnp.clip(jax.random.uniform(arg_keys[7], (2, M), jnp.float32, 0.5, 2.0), 0.5, 2.0)
    return dict(residual_cot=residual_cot, splat_weights=splat_weights, sample_cycle=sample_cycle, sample_pixel=sample_pixel, live_rows=live_rows, table_w=table_w, table_x=table_x, filters=filters)


corner_steps = ((0, 0), (0, 1), (1, 0), (1, 1))


def combine(with_w, with_x, pair_id, filters):
    row_width = with_w.shape[-1]
    num_sims = with_w.shape[0] // 8
    positions = jnp.arange(row_width, dtype=jnp.int32)
    first_part = positions < M - pair_id
    with_w = with_w.reshape(2, 2, num_sims, 2, row_width)
    with_x = with_x.reshape(2, 2, num_sims, 2, row_width)
    with_w = jnp.where(first_part, with_w[0], with_w[1])
    with_x = jnp.where(first_part, with_x[0], with_x[1])
    e_real = -(with_w[0, :, 0] - with_x[1, :, 1])
    e_imag = -(with_w[0, :, 1] + with_x[1, :, 0])
    b_real = -(with_w[1, :, 0] + with_x[0, :, 1])
    b_imag = -(with_w[1, :, 1] - with_x[0, :, 0])
    degree = jnp.where(first_part, pair_id + positions, positions - 1)
    degree = jnp.minimum(jnp.maximum(degree, 0), M - 1).astype(jnp.int32)
    filter_rows = jnp.take(filters, degree, axis=1)
    grad_real = filter_rows[0] * e_real + filter_rows[1] * b_real
    grad_imag = filter_rows[0] * e_imag + filter_rows[1] * b_imag
    return jnp.stack([grad_real, grad_imag], 1).astype(jnp.bfloat16)


def reference(residual_cot, splat_weights, sample_cycle, sample_pixel, live_rows, table_w, table_x, filters):
    pix_dev = NPHI // N_LON
    cycle_idx = sample_cycle.reshape(N_BAND, ROWS_DEV, N_LON, 128)
    pix_idx = sample_pixel.reshape(N_BAND, ROWS_DEV, N_LON, 128)
    band_ids = jnp.arange(N_BAND, dtype=jnp.int32)[:, None, None, None]
    lon_ids = jnp.arange(N_LON, dtype=jnp.int32)[None, None, :, None]
    row_ids = jnp.arange(ROWS_DEV, dtype=jnp.int32)[None, :, None, None]
    counts = live_rows.reshape(N_BAND, 1, N_LON, 1)
    live_mask = (row_ids < counts).astype(jnp.float32)
    values = residual_cot.reshape(2 * NSIM, N_BAND, ROWS_DEV, N_LON, 128)
    weights = splat_weights.reshape(4, N_BAND, ROWS_DEV, N_LON, 128)
    canvas = jnp.zeros((2 * NSIM, (NRING + 2) * NPHI), jnp.float32)
    for corner in range(4):
        cycle_step, pix_step = corner_steps[corner]
        cycle_at = band_ids * BAND_CYCLES + cycle_idx + cycle_step
        pix_at = (lon_ids * pix_dev - RIM + pix_idx + pix_step) % NPHI
        flat_index = (cycle_at * NPHI + pix_at).astype(jnp.int32).reshape(-1)
        amount = (values * (weights[corner] * live_mask)[None]).reshape(2 * NSIM, -1)
        canvas = canvas.at[:, flat_index].add(amount)
    sky_map = canvas.reshape(2 * NSIM, NRING + 2, NPHI)[:, 1:NRING + 1].astype(jnp.bfloat16)
    sky_map = sky_map.reshape(2 * NSIM * NRING, NPHI)
    pixels = jnp.arange(NPHI, dtype=jnp.int32)
    orders = jnp.arange(M, dtype=jnp.int32)
    turn_index = (pixels[:, None] * orders[None, :]) % NPHI
    angles = turn_index.astype(jnp.float32) * (2.0 * math.pi / NPHI)
    cos_table = jnp.cos(angles).astype(jnp.bfloat16)
    sin_table = (-jnp.sin(angles)).astype(jnp.bfloat16)
    norm_scale = NPHI ** -0.5
    real_part = jnp.dot(sky_map, cos_table, preferred_element_type=jnp.float32) * norm_scale
    imag_part = jnp.dot(sky_map, sin_table, preferred_element_type=jnp.float32) * norm_scale
    fourier = jnp.stack([real_part.reshape(2, NSIM, NRING, M), imag_part.reshape(2, NSIM, NRING, M)], 3)
    fourier = fourier.astype(jnp.bfloat16)
    pair_total = M // 2
    first_orders = fourier[..., :pair_total]
    second_orders = fourier[..., ::-1][..., :pair_total]
    stacked = jnp.stack([first_orders, second_orders], 0)
    stacked = jnp.transpose(stacked, (5, 0, 1, 2, 4, 3)).reshape(pair_total, 8 * NSIM, NRING)
    block_size = math.gcd(pair_total, 64)
    block_count = pair_total // block_size
    pair_ids = jnp.arange(pair_total, dtype=jnp.int32).reshape(block_count, block_size)

    def one_block(operands):
        rows_block, w_block, x_block, ids_block = operands
        with_w = jnp.einsum('kxr,kri->kxi', rows_block.astype(jnp.float32), w_block.astype(jnp.float32))
        with_x = jnp.einsum('kxr,kri->kxi', rows_block.astype(jnp.float32), x_block.astype(jnp.float32))
        return jax.vmap(combine, in_axes=(0, 0, 0, None))(with_w, with_x, ids_block, filters)

    result = lax.map(one_block, (stacked.reshape(block_count, block_size, 8 * NSIM, NRING),
                                 table_w.reshape(block_count, block_size, NRING, M + 1),
                                 table_x.reshape(block_count, block_size, NRING, M + 1),
                                 pair_ids))
    return result.reshape(pair_total, NSIM, 2, M + 1)
```

```python
import functools

import jax
import jax.numpy as jnp
import numpy as np
from jax import lax
from jax.experimental import pallas as pl
from jax.experimental.pallas import tpu as pltpu
from jax.sharding import PartitionSpec as P

BAND_CYCLES = 1
NPHI = 12288
M = 3072
RIM = 128
LANES = 128
FINE = 256
COARSE = NPHI // LANES
TURNS = M // COARSE
HALF = TURNS // 2
EXT_CYCLES = BAND_CYCLES + 2
F32 = jnp.float32
BF16 = jnp.bfloat16
VMEM = pl.BlockSpec(memory_space=pltpu.VMEM)
SMEM = pl.BlockSpec(memory_space=pltpu.SMEM)
HBM = pl.BlockSpec(memory_space=pltpu.HBM)


def split_bf16(array):
    high = array.astype(np.float32).astype(BF16)
    low = (array - high.astype(np.float64)).astype(np.float32).astype(BF16)
    return high, low


def coarse_table(pad_rows):
    row = np.arange(pad_rows)
    step = (2 * row[None, :] + np.arange(2)[:, None]).reshape(-1)
    m0 = np.arange(LANES)
    angle = 2 * np.pi * ((step[None, :] * m0[:, None]) % COARSE) / COARSE
    used = (m0 < COARSE)[:, None]
    high, low = split_bf16(np.concatenate([np.cos(angle) * used, -np.sin(angle) * used], 0))
    return np.concatenate([high, low, high], 1)


def twiddle_table(lon_count, pix_dev):
    l = np.arange(LANES)
    m0 = np.arange(LANES)
    table = np.zeros((lon_count, 2, LANES, LANES), np.float32)
    for j in range(lon_count):
        first = j * pix_dev - RIM
        angle = 2 * np.pi * (((l[None, :] + first) * m0[:, None]) % NPHI) / NPHI
        table[j, 0] = np.cos(angle) * NPHI**-0.5
        table[j, 1] = -np.sin(angle) * NPHI**-0.5
    return table


def fine_table(num_sims):
    l = np.arange(LANES)
    table = np.zeros((2, HALF, num_sims, 2, num_sims, 2, LANES))
    for side in range(2):
        for d in range(HALF):
            m1 = d if side == 0 else TURNS - 1 - d
            angle = 2 * np.pi * ((l * m1) % LANES) / LANES
            for s in range(num_sims):
                table[side, d, s, 0, s, 0] = np.cos(angle)
                table[side, d, s, 0, s, 1] = np.sin(angle)
                table[side, d, s, 1, s, 0] = -np.sin(angle)
                table[side, d, s, 1, s, 1] = np.cos(angle)
    return split_bf16(table.reshape(4 * HALF * num_sims, 2 * num_sims * LANES))[0]


def analyse_kernel(
    live_ref, value_ref, weight_ref, cycle_ref, pixel_ref, coarse_hbm, twiddle_hbm, fine_hbm,
    out_ref, amount, index, left, right, coarse_ref, twiddle_ref, fine_ref, sems, *, pad_rows,
):
    tables = [
        pltpu.make_async_copy(coarse_hbm, coarse_ref, sems.at[0]),
        pltpu.make_async_copy(twiddle_hbm.at[lax.axis_index("lon")], twiddle_ref, sems.at[1]),
        pltpu.make_async_copy(fine_hbm, fine_ref, sems.at[2]),
    ]
    for copy in tables:
        copy.start()
    num_sims, rows = value_ref.shape[1:3]
    maps = num_sims * EXT_CYCLES
    alive = lax.broadcasted_iota(jnp.int32, (rows, LANES), 0) < live_ref[0]
    cycle = cycle_ref[...]
    for dp in range(2):
        pixel = pixel_ref[...] + dp
        index[0, dp] = (pixel >> 8).astype(F32)
        index[1, dp] = (pixel & (FINE - 1)).astype(F32)
        for s in range(num_sims):
            value = jnp.where(alive, value_ref[0, s], 0.0)
            here = value * weight_ref[dp]
            above = value * weight_ref[2 + dp]
            for c in range(EXT_CYCLES):
                amount[s * EXT_CYCLES + c, dp] = jnp.where(
                    cycle == c, here, jnp.where(cycle == c - 1, above, 0.0)
                )
    row_at = lax.broadcasted_iota(jnp.int32, (pad_rows, LANES), 0).astype(F32).astype(BF16)
    fine_at = lax.broadcasted_iota(jnp.int32, (FINE, LANES), 0).astype(F32).astype(BF16)
    one, zero = jnp.ones((), BF16), jnp.zeros((), BF16)

    def all_rows(ref, n, dp, k, count):
        row = jnp.broadcast_to(ref[n, dp, k : k + 1, :], (16, LANES)).astype(BF16)
        return jnp.concatenate([row] * (count // 16), 0)

    for k in range(rows):
        for dp in range(2):
            here = slice(FINE * k + LANES * dp, FINE * k + LANES * (dp + 1))
            hit = row_at == all_rows(index, 0, dp, k, pad_rows)
            for n in range(maps):
                left[n * pad_rows : (n + 1) * pad_rows, here] = jnp.where(
                    hit, all_rows(amount, n, dp, k, pad_rows), zero
                )
            right[:, here] = jnp.where(fine_at == all_rows(index, 1, dp, k, FINE), one, zero)
    dims = (((1,), (1,)), ((), ()))
    canvas = lax.dot_general(left[...], right[...], dims, preferred_element_type=F32)
    canvas = jnp.concatenate(
        [
            jnp.concatenate(
                [
                    canvas[n * pad_rows : (n + 1) * pad_rows, b * LANES : (b + 1) * LANES]
                    for n in range(maps)
                ],
                1,
            )
            for b in range(2)
        ],
        0,
    )
    high = canvas.astype(BF16)
    low = (canvas - high.astype(F32)).astype(BF16)
    for copy in tables:
        copy.wait()
    coarse = jnp.dot(
        coarse_ref[...], jnp.concatenate([high, high, low], 0), preferred_element_type=F32
    )
    turn_re, turn_im = twiddle_ref[0], twiddle_ref[1]
    blocks = []
    for c in range(EXT_CYCLES):
        lanes = []
        for s in range(num_sims):
            n = s * EXT_CYCLES + c
            real = coarse[:LANES, n * LANES : (n + 1) * LANES]
            imag = coarse[LANES:, n * LANES : (n + 1) * LANES]
            lanes += [real * turn_re - imag * turn_im, real * turn_im + imag * turn_re]
        blocks.append(jnp.concatenate(lanes, 1))
    turned = jnp.concatenate(blocks, 0).astype(BF16)
    modes = lax.dot_general(fine_ref[...], turned, dims, preferred_element_type=F32)
    half = modes.shape[0] // 2
    modes = jnp.concatenate([modes[:half], modes[half:]], 1).astype(BF16)
    out_ref[...] = modes.reshape(out_ref.shape)


def analyse(live_rows, values, weights, cycle, pixel, pix_dev, lon_count):
    num_sims, rows = values.shape[1:3]
    pad_rows = -(-(pix_dev + 2 * RIM) // FINE // 16) * 16
    maps = num_sims * EXT_CYCLES
    coarse, fine = coarse_table(pad_rows), fine_table(num_sims)
    twiddle = twiddle_table(lon_count, pix_dev)
    out_shape = (HALF, 2 * num_sims, 2 * EXT_CYCLES * LANES)

    def whole(shape):
        return pl.BlockSpec(shape, lambda i: (0,) * len(shape))

    return pl.pallas_call(
        functools.partial(analyse_kernel, pad_rows=pad_rows),
        grid=(1,),
        in_specs=[
            SMEM,
            whole(values.shape),
            whole(weights.shape),
            whole(cycle.shape),
            whole(pixel.shape),
            HBM,
            HBM,
            HBM,
        ],
        out_specs=whole(out_shape),
        scratch_shapes=[
            pltpu.VMEM((maps, 2, rows, LANES), F32),
            pltpu.VMEM((2, 2, rows, LANES), F32),
            pltpu.VMEM((maps * pad_rows, rows * FINE), BF16),
            pltpu.VMEM((FINE, rows * FINE), BF16),
            pltpu.VMEM(coarse.shape, BF16),
            pltpu.VMEM(twiddle.shape[1:], F32),
            pltpu.VMEM(fine.shape, BF16),
            pltpu.SemaphoreType.DMA((3,)),
        ],
        out_shape=jax.ShapeDtypeStruct(out_shape, BF16),
        compiler_params=pltpu.CompilerParams(vmem_limit_bytes=56 << 20),
    )(
        live_rows, values, weights, cycle, pixel,
        jnp.asarray(coarse), jnp.asarray(twiddle), jnp.asarray(fine),
    )


def first_pair_here(per_pair):
    place = lax.axis_index("band") * lax.axis_size("lon") + lax.axis_index("lon")
    return (place * lax.axis_size("pol") + lax.axis_index("pol")) * per_pair


def spread_kernel(filters_ref, out_ref, *, per_pair):
    wide = out_ref.shape[3]
    first_pair = first_pair_here(per_pair)
    second = lax.broadcasted_iota(jnp.int32, (8, wide), 0) // 4
    for f in range(2):
        full = jnp.concatenate([filters_ref[f : f + 1, :], jnp.zeros((1, wide - M), F32)], 1)
        full = jnp.broadcast_to(full, (8, wide))
        ahead = jnp.where(second == 1, pltpu.roll(full, wide - 1, 1), full)
        out_ref[0, f] = pltpu.roll(ahead, wide - first_pair, 1)
        out_ref[1, f] = pltpu.roll(full, 1, 1)


def spread_filters(filters, per_pair):
    wide = M + FINE + -(-per_pair // LANES) * LANES
    return pl.pallas_call(
        functools.partial(spread_kernel, per_pair=per_pair),
        in_specs=[VMEM],
        out_specs=VMEM,
        out_shape=jax.ShapeDtypeStruct((2, 2, 8, wide), F32),
        compiler_params=pltpu.CompilerParams(vmem_limit_bytes=8 << 20),
        cost_estimate=pl.CostEstimate(flops=400 * wide, bytes_accessed=160 * wide, transcendentals=0),
    )(filters)


def grouping(per_pair, cycles):
    group = 2
    while per_pair % (2 * group) == 0 and 2 * group * cycles <= LANES:
        group *= 2
    return group, -(-group * cycles // LANES) * LANES


def swap_parts(array):
    even = lax.broadcasted_iota(jnp.int32, array.shape, 0) % 2 == 0
    return jnp.where(even, pltpu.roll(array, 7, 0), pltpu.roll(array, 1, 0))


def contract_kernel(
    modes_ref, spread_ref, w_hbm, x_hbm, out_ref, modes, factors, held, w_ref, x_ref, sems, *, direct
):
    per_pair, cycles, row_width = w_ref.shape
    group, pad_depth = grouping(per_pair, cycles)
    groups, depth, half = per_pair // group, group * cycles, 4 * group
    tables = []
    for g in range(groups):
        part = pl.ds(g * group, group)
        tables.append(
            [
                pltpu.make_async_copy(w_hbm.at[part], w_ref.at[part], sems.at[g, 0]),
                pltpu.make_async_copy(x_hbm.at[part], x_ref.at[part], sems.at[g, 1]),
            ]
        )
        for copy in tables[-1]:
            copy.start()
    for comp in range(2):
        for side in range(2):
            for r in range(cycles):
                if direct:
                    total = jnp.zeros((4, LANES), F32)
                    lons = modes_ref.shape[0] // (2 * cycles)
                    for c in range(EXT_CYCLES):
                        band = r + 1 - c
                        if 0 <= band < cycles:
                            for j in range(lons):
                                lane = (side * EXT_CYCLES + c) * LANES
                                total += modes_ref[
                                    (band * lons + j) * 2 + comp, :, lane : lane + LANES
                                ].astype(F32)
                    total = total.astype(BF16).astype(F32)
                    total = jnp.concatenate([total, total], 0)
                else:
                    total = modes_ref[comp, side, r]
                modes[comp, side, r] = total

    lane = lax.broadcasted_iota(jnp.int32, (8, LANES), 1)
    sign = jnp.where(lax.broadcasted_iota(jnp.int32, (8, pad_depth), 0) % 2 == 0, 1.0, -1.0)
    own = (
        lax.broadcasted_iota(jnp.int32, (half, pad_depth), 0) // 4
        == lax.broadcasted_iota(jnp.int32, (half, pad_depth), 1) // cycles
    )
    copies = []
    for g in range(groups):
        for side in range(2):
            spread = []
            for comp in range(2):
                parts = []
                for first in range(0, pad_depth, LANES):
                    at = jnp.minimum(g * group + (first + lane) // cycles, per_pair - 1)
                    if direct and side == 1:
                        at = per_pair - 1 - at
                    value = jnp.zeros((8, LANES), F32)
                    for r in range(cycles):
                        taken = jnp.take_along_axis(
                            modes[comp, side, r], at, axis=1, mode="promise_in_bounds"
                        )
                        value = jnp.where((first + lane) % cycles == r, taken, value)
                    parts.append(value)
                spread.append(jnp.concatenate(parts, 1) if len(parts) > 1 else parts[0])
            q, u = spread
            pairs = ((-q, sign * swap_parts(u)), (-u, -sign * swap_parts(q)))
            for f, bases in enumerate(pairs):
                for n, base in enumerate(bases):
                    full = jnp.where(own, jnp.tile(base, (half // 8, 1)), 0.0).astype(BF16)
                    factors[
                        g, side, f * half : (f + 1) * half, n * pad_depth : (n + 1) * pad_depth
                    ] = full

    for g in range(groups):
        first_pair = first_pair_here(per_pair) + g * group
        for copy in tables[g]:
            copy.wait()

        def table_rows(cols):
            rows = []
            for ref in (w_ref, x_ref):
                rows.append(ref[g * group : (g + 1) * group, :, cols].reshape(depth, -1))
                if depth < pad_depth:
                    rows.append(jnp.zeros((pad_depth - depth, rows[0].shape[1]), BF16))
            return jnp.concatenate(rows, 0)

        def filtered(rows, side, start, width):
            both = jnp.dot(factors[g, side], rows, preferred_element_type=F32)
            near = 1 - side
            total = []
            source = [spread_ref[side, f, :, pl.ds(start, FINE + LANES)] for f in range(2)]
            for a in range(half // 8):
                shift = 2 * a + g * group
                e, b = (
                    pltpu.roll(source[f], (FINE + LANES) - shift * near, 1)[:, :width] for f in range(2)
                )
                total.append(e * both[8 * a : 8 * a + 8] + b * both[half + 8 * a : half + 8 * a + 8])
            return jnp.concatenate(total, 0)

        def put(total, cols):
            held[g, :, :, :, cols] = total.astype(BF16).reshape(group, 2, 2, -1)

        for start in range(0, row_width, FINE):
            cols = slice(start, min(start + FINE, row_width))
            side = (start >= M - first_pair).astype(jnp.int32)
            put(filtered(table_rows(cols), side, start, cols.stop - start), cols)
        start = pl.multiple_of((M - 1 - first_pair) // FINE * FINE, FINE)
        cols = pl.ds(start, FINE)
        rows = table_rows(cols)
        pair = first_pair + lax.broadcasted_iota(jnp.int32, (half, FINE), 0) // 4
        at = start + lax.broadcasted_iota(jnp.int32, (half, FINE), 1)
        near, far = (filtered(rows, side, start, FINE) for side in range(2))
        put(jnp.where(at < M - pair, near, far), cols)
        copy = pltpu.make_async_copy(
            held.at[g], out_ref.at[pl.ds(g * group, group)], sems.at[g, 2]
        )
        copy.start()
        copies.append(copy)
    for copy in copies:
        copy.wait()


def contract(modes, spread, table_w, table_x, direct):
    per_pair, cycles, row_width = table_w.shape
    group, pad_depth = grouping(per_pair, cycles)
    groups = per_pair // group
    return pl.pallas_call(
        functools.partial(contract_kernel, direct=direct),
        in_specs=[VMEM, VMEM, HBM, HBM],
        out_specs=HBM,
        out_shape=jax.ShapeDtypeStruct((per_pair, 2, 2, row_width), BF16),
        scratch_shapes=[
            pltpu.VMEM((2, 2, cycles, 8, LANES), F32),
            pltpu.VMEM((groups, 2, 8 * group, 2 * pad_depth), BF16),
            pltpu.VMEM((groups, group, 2, 2, row_width), BF16),
            pltpu.VMEM(table_w.shape, BF16),
            pltpu.VMEM(table_x.shape, BF16),
            pltpu.SemaphoreType.DMA((groups, 3)),
        ],
        compiler_params=pltpu.CompilerParams(vmem_limit_bytes=56 << 20),
    )(modes, spread, table_w, table_x)


def by_owner(payload, per_pair):
    split = COARSE // per_pair
    parts = payload.reshape(HALF, 4, 2, EXT_CYCLES, LANES)[..., :COARSE]
    parts = jnp.stack([parts[:, :, 0], parts[:, :, 1, :, ::-1]], 2)
    parts = parts.reshape(HALF, 4, 2, EXT_CYCLES, split, per_pair)
    parts = jnp.transpose(parts, (0, 4, 1, 2, 3, 5))
    return parts.reshape(HALF * split, 4, 2, EXT_CYCLES, per_pair)


def sum_sources(received, bands, lons):
    per_pair = received.shape[-1]
    parts = received.astype(F32).reshape(bands, lons, 2, 4, 2, EXT_CYCLES, per_pair).sum(1)
    parts = jnp.pad(parts, ((1, 1), (0, 0), (0, 0), (0, 0), (0, 0), (0, 0)))
    total = sum(parts[2 - c : 2 - c + bands, :, :, :, c] for c in range(EXT_CYCLES))
    total = jnp.transpose(total, (1, 3, 0, 2, 4)).astype(BF16).astype(F32)
    total = jnp.concatenate([total, total], 3)
    return jnp.pad(total, ((0, 0),) * 4 + ((0, LANES - per_pair),))


def body(
    residual_cot, splat_weights, sample_cycle, sample_pixel, live_rows, table_w, table_x, filters
):
    bands = lax.axis_size("band")
    lons = lax.axis_size("lon")
    owners = ("band", "lon", "pol")
    per_pair = table_w.shape[0]
    payload = analyse(
        live_rows, residual_cot, splat_weights, sample_cycle, sample_pixel, NPHI // lons, lons
    )
    direct = per_pair == COARSE
    if not direct:
        payload = by_owner(payload, per_pair)
    modes = lax.all_to_all(payload, owners, 0, 0, tiled=True)
    if not direct:
        modes = sum_sources(modes, bands, lons)
    spread = spread_filters(filters, per_pair)
    return contract(modes, spread, table_w, table_x, direct)


def solution(mesh):
    in_specs = (
        P("pol", "sky", "band", "lon"),
        P("sky", "band", "lon"),
        P(("sky", "band"), "lon"),
        P(("sky", "band"), "lon"),
        P(("sky", "band", "lon")),
        P(("band", "lon", "pol"), None, None),
        P(("band", "lon", "pol"), None, None),
        P(),
    )
    out_specs = P(("band", "lon", "pol"), "sky", None, None)
    return jax.shard_map(body, mesh=mesh, in_specs=in_specs, out_specs=out_specs, check_vma=False)
```

```python
import functools

import jax
import jax.numpy as jnp
import numpy as np
from jax import lax
from jax.experimental import pallas as pl
from jax.experimental.pallas import tpu as pltpu
from jax.sharding import PartitionSpec as P

BAND_CYCLES = 1
NPHI = 12288
M = 3072
RIM = 128
LANES = 128
FINE = 256
PIECE = 1024
COARSE = NPHI // LANES
TURNS = M // COARSE
HALF = TURNS // 2
EXT_CYCLES = BAND_CYCLES + 2
F32 = jnp.float32
BF16 = jnp.bfloat16
VMEM = pl.BlockSpec(memory_space=pltpu.VMEM)
SMEM = pl.BlockSpec(memory_space=pltpu.SMEM)
HBM = pl.BlockSpec(memory_space=pltpu.HBM)


def split_bf16(array):
    high = array.astype(np.float32).astype(BF16)
    low = (array - high.astype(np.float64)).astype(np.float32).astype(BF16)
    return high, low


def coarse_table(pad_rows):
    row = np.arange(pad_rows)
    step = (2 * row[None, :] + np.arange(2)[:, None]).reshape(-1)
    m0 = np.arange(LANES)
    angle = 2 * np.pi * ((step[None, :] * m0[:, None]) % COARSE) / COARSE
    used = (m0 < COARSE)[:, None]
    high, low = split_bf16(np.concatenate([np.cos(angle) * used, -np.sin(angle) * used], 0))
    return np.concatenate([high, low, high], 1)


def twiddle_table(lon_count, pix_dev):
    l = np.arange(LANES)
    m0 = np.arange(LANES)
    table = np.zeros((lon_count, 2, LANES, LANES), np.float32)
    for j in range(lon_count):
        first = j * pix_dev - RIM
        angle = 2 * np.pi * (((l[None, :] + first) * m0[:, None]) % NPHI) / NPHI
        table[j, 0] = np.cos(angle) * NPHI**-0.5
        table[j, 1] = -np.sin(angle) * NPHI**-0.5
    return table


def fine_table(num_sims):
    l = np.arange(LANES)
    table = np.zeros((2, HALF, num_sims, 2, num_sims, 2, LANES))
    for side in range(2):
        for d in range(HALF):
            m1 = d if side == 0 else TURNS - 1 - d
            angle = 2 * np.pi * ((l * m1) % LANES) / LANES
            for s in range(num_sims):
                table[side, d, s, 0, s, 0] = np.cos(angle)
                table[side, d, s, 0, s, 1] = np.sin(angle)
                table[side, d, s, 1, s, 0] = -np.sin(angle)
                table[side, d, s, 1, s, 1] = np.cos(angle)
    return split_bf16(table.reshape(4 * HALF * num_sims, 2 * num_sims * LANES))[0]


def analyse_kernel(
    live_ref, value_ref, weight_ref, cycle_ref, pixel_ref, coarse_hbm, twiddle_hbm, fine_hbm,
    out_ref, amount, index, left, right, coarse_ref, twiddle_ref, fine_ref, sems, *, pad_rows,
):
    tables = [
        pltpu.make_async_copy(coarse_hbm, coarse_ref, sems.at[0]),
        pltpu.make_async_copy(twiddle_hbm.at[lax.axis_index("lon")], twiddle_ref, sems.at[1]),
        pltpu.make_async_copy(fine_hbm, fine_ref, sems.at[2]),
    ]
    for copy in tables:
        copy.start()
    num_sims, rows = value_ref.shape[1:3]
    maps = num_sims * EXT_CYCLES
    alive = lax.broadcasted_iota(jnp.int32, (rows, LANES), 0) < live_ref[0]
    cycle = cycle_ref[...]
    for dp in range(2):
        pixel = pixel_ref[...] + dp
        index[0, dp] = (pixel >> 8).astype(F32)
        index[1, dp] = (pixel & (FINE - 1)).astype(F32)
        for s in range(num_sims):
            value = jnp.where(alive, value_ref[0, s], 0.0)
            here = value * weight_ref[dp]
            above = value * weight_ref[2 + dp]
            for c in range(EXT_CYCLES):
                amount[s * EXT_CYCLES + c, dp] = jnp.where(
                    cycle == c, here, jnp.where(cycle == c - 1, above, 0.0)
                )
    row_at = lax.broadcasted_iota(jnp.int32, (pad_rows, LANES), 0).astype(F32).astype(BF16)
    fine_at = lax.broadcasted_iota(jnp.int32, (FINE, LANES), 0).astype(F32).astype(BF16)
    one, zero = jnp.ones((), BF16), jnp.zeros((), BF16)

    def all_rows(ref, n, dp, k, count):
        row = jnp.broadcast_to(ref[n, dp, k : k + 1, :], (16, LANES)).astype(BF16)
        return jnp.concatenate([row] * (count // 16), 0)

    for k in range(rows):
        for dp in range(2):
            here = slice(FINE * k + LANES * dp, FINE * k + LANES * (dp + 1))
            hit = row_at == all_rows(index, 0, dp, k, pad_rows)
            for n in range(maps):
                left[n * pad_rows : (n + 1) * pad_rows, here] = jnp.where(
                    hit, all_rows(amount, n, dp, k, pad_rows), zero
                )
            right[:, here] = jnp.where(fine_at == all_rows(index, 1, dp, k, FINE), one, zero)
    dims = (((1,), (1,)), ((), ()))
    canvas = lax.dot_general(left[...], right[...], dims, preferred_element_type=F32)
    canvas = jnp.concatenate(
        [
            jnp.concatenate(
                [
                    canvas[n * pad_rows : (n + 1) * pad_rows, b * LANES : (b + 1) * LANES]
                    for n in range(maps)
                ],
                1,
            )
            for b in range(2)
        ],
        0,
    )
    high = canvas.astype(BF16)
    low = (canvas - high.astype(F32)).astype(BF16)
    for copy in tables:
        copy.wait()
    coarse = jnp.dot(
        coarse_ref[...], jnp.concatenate([high, high, low], 0), preferred_element_type=F32
    )
    turn_re, turn_im = twiddle_ref[0], twiddle_ref[1]
    blocks = []
    for c in range(EXT_CYCLES):
        lanes = []
        for s in range(num_sims):
            n = s * EXT_CYCLES + c
            real = coarse[:LANES, n * LANES : (n + 1) * LANES]
            imag = coarse[LANES:, n * LANES : (n + 1) * LANES]
            lanes += [real * turn_re - imag * turn_im, real * turn_im + imag * turn_re]
        blocks.append(jnp.concatenate(lanes, 1))
    turned = jnp.concatenate(blocks, 0).astype(BF16)
    modes = lax.dot_general(fine_ref[...], turned, dims, preferred_element_type=F32)
    half = modes.shape[0] // 2
    modes = jnp.concatenate([modes[:half], modes[half:]], 1).astype(BF16)
    out_ref[...] = modes.reshape(out_ref.shape)


def analyse(live_rows, values, weights, cycle, pixel, pix_dev, lon_count):
    num_sims, rows = values.shape[1:3]
    pad_rows = -(-(pix_dev + 2 * RIM) // FINE // 16) * 16
    maps = num_sims * EXT_CYCLES
    coarse, fine = coarse_table(pad_rows), fine_table(num_sims)
    twiddle = twiddle_table(lon_count, pix_dev)
    out_shape = (HALF, 2 * num_sims, 2 * EXT_CYCLES * LANES)

    def whole(shape):
        return pl.BlockSpec(shape, lambda i: (0,) * len(shape))

    return pl.pallas_call(
        functools.partial(analyse_kernel, pad_rows=pad_rows),
        grid=(1,),
        in_specs=[
            SMEM,
            whole(values.shape),
            whole(weights.shape),
            whole(cycle.shape),
            whole(pixel.shape),
            HBM,
            HBM,
            HBM,
        ],
        out_specs=whole(out_shape),
        scratch_shapes=[
            pltpu.VMEM((maps, 2, rows, LANES), F32),
            pltpu.VMEM((2, 2, rows, LANES), F32),
            pltpu.VMEM((maps * pad_rows, rows * FINE), BF16),
            pltpu.VMEM((FINE, rows * FINE), BF16),
            pltpu.VMEM(coarse.shape, BF16),
            pltpu.VMEM(twiddle.shape[1:], F32),
            pltpu.VMEM(fine.shape, BF16),
            pltpu.SemaphoreType.DMA((3,)),
        ],
        out_shape=jax.ShapeDtypeStruct(out_shape, BF16),
        compiler_params=pltpu.CompilerParams(vmem_limit_bytes=56 << 20),
    )(
        live_rows, values, weights, cycle, pixel,
        jnp.asarray(coarse), jnp.asarray(twiddle), jnp.asarray(fine),
    )


def first_pair_here(per_pair):
    place = lax.axis_index("band") * lax.axis_size("lon") + lax.axis_index("lon")
    return (place * lax.axis_size("pol") + lax.axis_index("pol")) * per_pair


def spread_kernel(filters_ref, out_ref):
    groups, _, group, wide = out_ref.shape
    first_pair = first_pair_here(groups * group)
    at = lax.broadcasted_iota(jnp.int32, (8, wide), 1)
    row = lax.broadcasted_iota(jnp.int32, (8, wide), 0)
    for f in range(2):
        full = jnp.concatenate([filters_ref[f : f + 1, :], jnp.zeros((1, wide - M), F32)], 1)
        full = jnp.broadcast_to(full, (8, wide))
        behind = pltpu.roll(full, 1, 1)
        ahead = full
        for bit in (1, 2, 4):
            ahead = jnp.where(row & bit != 0, pltpu.roll(ahead, wide - bit, 1), ahead)
        ahead = pltpu.roll(ahead, wide - first_pair, 1)
        for g in range(groups):
            for a in range(0, group, 8):
                first = g * group + a
                here = pltpu.roll(ahead, wide - first, 1) if first else ahead
                here = jnp.where(at < M - first_pair - first - row, here, behind)
                count = min(8, group - a)
                out_ref[g, f, a : a + count, :] = here[:count]


def spread_filters(filters, per_pair, cycles):
    group = grouping(per_pair, cycles)[0]
    wide = -(-(M + 1) // LANES) * LANES
    return pl.pallas_call(
        spread_kernel,
        in_specs=[VMEM],
        out_specs=VMEM,
        out_shape=jax.ShapeDtypeStruct((per_pair // group, 2, group, wide), F32),
        compiler_params=pltpu.CompilerParams(vmem_limit_bytes=8 << 20),
        cost_estimate=pl.CostEstimate(
            flops=20 * per_pair * wide, bytes_accessed=8 * per_pair * wide, transcendentals=0
        ),
    )(filters)


def grouping(per_pair, cycles):
    group = 2
    while per_pair % (2 * group) == 0 and 2 * group * cycles <= LANES:
        group *= 2
    return group, -(-group * cycles // LANES) * LANES


def swap_parts(array):
    even = lax.broadcasted_iota(jnp.int32, array.shape, 0) % 2 == 0
    return jnp.where(even, pltpu.roll(array, 7, 0), pltpu.roll(array, 1, 0))


def contract_kernel(
    modes_ref, spread_ref, w_hbm, x_hbm, out_ref,
    modes, factors, held, w_ref, x_ref, sems, *, direct,
):
    per_pair, cycles, row_width = w_ref.shape
    group, pad_depth = grouping(per_pair, cycles)
    groups, depth, half = per_pair // group, group * cycles, 4 * group
    tables = []
    for g in range(groups):
        part = pl.ds(g * group, group)
        tables.append(
            [
                pltpu.make_async_copy(w_hbm.at[part], w_ref.at[part], sems.at[g, 0]),
                pltpu.make_async_copy(x_hbm.at[part], x_ref.at[part], sems.at[g, 1]),
            ]
        )
        for copy in tables[-1]:
            copy.start()
    for comp in range(2):
        for side in range(2):
            for r in range(cycles):
                if direct:
                    total = jnp.zeros((4, LANES), F32)
                    lons = modes_ref.shape[0] // (2 * cycles)
                    for c in range(EXT_CYCLES):
                        band = r + 1 - c
                        if 0 <= band < cycles:
                            for j in range(lons):
                                lane = (side * EXT_CYCLES + c) * LANES
                                total += modes_ref[
                                    (band * lons + j) * 2 + comp, :, lane : lane + LANES
                                ].astype(F32)
                    total = total.astype(BF16).astype(F32)
                    total = jnp.concatenate([total, total], 0)
                else:
                    total = modes_ref[comp, side, r]
                modes[comp, side, r] = total

    lane = lax.broadcasted_iota(jnp.int32, (8, LANES), 1)
    sign = jnp.where(lax.broadcasted_iota(jnp.int32, (8, pad_depth), 0) % 2 == 0, 1.0, -1.0)
    own = (
        lax.broadcasted_iota(jnp.int32, (half, pad_depth), 0) // 4
        == lax.broadcasted_iota(jnp.int32, (half, pad_depth), 1) // cycles
    )
    copies = []
    for g in range(groups):
        for side in range(2):
            spread = []
            for comp in range(2):
                parts = []
                for first in range(0, pad_depth, LANES):
                    at = jnp.minimum(g * group + (first + lane) // cycles, per_pair - 1)
                    if direct and side == 1:
                        at = per_pair - 1 - at
                    value = jnp.zeros((8, LANES), F32)
                    for r in range(cycles):
                        taken = jnp.take_along_axis(
                            modes[comp, side, r], at, axis=1, mode="promise_in_bounds"
                        )
                        value = jnp.where((first + lane) % cycles == r, taken, value)
                    parts.append(value)
                spread.append(jnp.concatenate(parts, 1) if len(parts) > 1 else parts[0])
            q, u = spread
            pairs = ((-q, sign * swap_parts(u)), (-u, -sign * swap_parts(q)))
            for f, bases in enumerate(pairs):
                for n, base in enumerate(bases):
                    full = jnp.where(own, jnp.tile(base, (half // 8, 1)), 0.0).astype(BF16)
                    factors[
                        g, side, f * half : (f + 1) * half, n * pad_depth : (n + 1) * pad_depth
                    ] = full

    for g in range(groups):
        first_pair = first_pair_here(per_pair) + g * group
        for copy in tables[g]:
            copy.wait()

        def table_rows(cols):
            rows = []
            for ref in (w_ref, x_ref):
                rows.append(ref[g * group : (g + 1) * group, :, cols].reshape(depth, -1))
                if depth < pad_depth:
                    rows.append(jnp.zeros((pad_depth - depth, rows[0].shape[1]), BF16))
            return jnp.concatenate(rows, 0)

        def filtered(rows, side, cols):
            both = jnp.dot(factors[g, side], rows, preferred_element_type=F32)
            width = both.shape[1]
            total = []
            for a in range(half // 8):
                pair = 2 * a
                e, b = (
                    jnp.concatenate(
                        [
                            jnp.broadcast_to(spread_ref[g, f, pair + n : pair + n + 1, cols], (4, width))
                            for n in range(2)
                        ],
                        0,
                    )
                    for f in range(2)
                )
                total.append(e * both[8 * a : 8 * a + 8] + b * both[half + 8 * a : half + 8 * a + 8])
            return jnp.concatenate(total, 0)

        def put(total, slot, cols):
            held[slot, :, :, :, cols] = total.astype(BF16).reshape(group, 2, 2, -1)

        mixed = pl.multiple_of((M - 1 - first_pair) // FINE * FINE, FINE)
        cols = pl.ds(mixed, FINE)
        rows = table_rows(cols)
        pair = first_pair + lax.broadcasted_iota(jnp.int32, (half, FINE), 0) // 4
        at = mixed + lax.broadcasted_iota(jnp.int32, (half, FINE), 1)
        near, far = (filtered(rows, side, cols) for side in range(2))
        put(jnp.where(at < M - pair, near, far), g, cols)
        sent = 0
        for start in range(0, row_width, FINE):
            stop = min(start + FINE, row_width)
            cols = slice(start, stop)
            side = (start >= M - first_pair).astype(jnp.int32)
            slot = jnp.where(start == mixed, groups, g)
            put(filtered(table_rows(cols), side, cols), slot, cols)
            if stop == row_width or (stop % PIECE == 0 and row_width - stop > FINE):
                piece = pl.ds(sent, stop - sent)
                copy = pltpu.make_async_copy(
                    held.at[g, :, :, :, piece],
                    out_ref.at[pl.ds(g * group, group), :, :, piece],
                    sems.at[g, 2 + sent // PIECE],
                )
                copy.start()
                copies.append(copy)
                sent = stop
    for copy in copies:
        copy.wait()


def contract(modes, spread, table_w, table_x, direct):
    per_pair, cycles, row_width = table_w.shape
    group, pad_depth = grouping(per_pair, cycles)
    groups = per_pair // group
    return pl.pallas_call(
        functools.partial(contract_kernel, direct=direct),
        in_specs=[VMEM, VMEM, HBM, HBM],
        out_specs=HBM,
        out_shape=jax.ShapeDtypeStruct((per_pair, 2, 2, row_width), BF16),
        scratch_shapes=[
            pltpu.VMEM((2, 2, cycles, 8, LANES), F32),
            pltpu.VMEM((groups, 2, 8 * group, 2 * pad_depth), BF16),
            pltpu.VMEM((groups + 1, group, 2, 2, row_width), BF16),
            pltpu.VMEM(table_w.shape, BF16),
            pltpu.VMEM(table_x.shape, BF16),
            pltpu.SemaphoreType.DMA((groups, 2 + -(-row_width // PIECE))),
        ],
        compiler_params=pltpu.CompilerParams(vmem_limit_bytes=50 << 20),
    )(modes, spread, table_w, table_x)


def by_owner(payload, per_pair):
    split = COARSE // per_pair
    parts = payload.reshape(HALF, 4, 2, EXT_CYCLES, LANES)[..., :COARSE]
    parts = jnp.stack([parts[:, :, 0], parts[:, :, 1, :, ::-1]], 2)
    parts = parts.reshape(HALF, 4, 2, EXT_CYCLES, split, per_pair)
    parts = jnp.transpose(parts, (0, 4, 1, 2, 3, 5))
    return parts.reshape(HALF * split, 4, 2, EXT_CYCLES, per_pair)


def sum_sources(received, bands, lons):
    per_pair = received.shape[-1]
    parts = received.astype(F32).reshape(bands, lons, 2, 4, 2, EXT_CYCLES, per_pair).sum(1)
    parts = jnp.pad(parts, ((1, 1), (0, 0), (0, 0), (0, 0), (0, 0), (0, 0)))
    total = sum(parts[2 - c : 2 - c + bands, :, :, :, c] for c in range(EXT_CYCLES))
    total = jnp.transpose(total, (1, 3, 0, 2, 4)).astype(BF16).astype(F32)
    total = jnp.concatenate([total, total], 3)
    return jnp.pad(total, ((0, 0),) * 4 + ((0, LANES - per_pair),))


def body(
    residual_cot, splat_weights, sample_cycle, sample_pixel, live_rows, table_w, table_x, filters
):
    bands = lax.axis_size("band")
    lons = lax.axis_size("lon")
    owners = ("band", "lon", "pol")
    per_pair = table_w.shape[0]
    payload = analyse(
        live_rows, residual_cot, splat_weights, sample_cycle, sample_pixel, NPHI // lons, lons
    )
    direct = per_pair == COARSE
    if not direct:
        payload = by_owner(payload, per_pair)
    modes = lax.all_to_all(payload, owners, 0, 0, tiled=True)
    if not direct:
        modes = sum_sources(modes, bands, lons)
    spread = spread_filters(filters, per_pair, table_w.shape[1])
    return contract(modes, spread, table_w, table_x, direct)


def solution(mesh):
    in_specs = (
        P("pol", "sky", "band", "lon"),
        P("sky", "band", "lon"),
        P(("sky", "band"), "lon"),
        P(("sky", "band"), "lon"),
        P(("sky", "band", "lon")),
        P(("band", "lon", "pol"), None, None),
        P(("band", "lon", "pol"), None, None),
        P(),
    )
    out_specs = P(("band", "lon", "pol"), "sky", None, None)
    return jax.shard_map(body, mesh=mesh, in_specs=in_specs, out_specs=out_specs, check_vma=False)
```

```python
import functools

import jax
import jax.numpy as jnp
import numpy as np
from jax import lax
from jax.experimental import pallas as pl
from jax.experimental.pallas import tpu as pltpu
from jax.sharding import PartitionSpec as P

BAND_CYCLES = 1
NPHI = 12288
M = 3072
RIM = 128
LANES = 128
FINE = 256
PIECE = 1024
COARSE = NPHI // LANES
TURNS = M // COARSE
HALF = TURNS // 2
EXT_CYCLES = BAND_CYCLES + 2
F32 = jnp.float32
BF16 = jnp.bfloat16
VMEM = pl.BlockSpec(memory_space=pltpu.VMEM)
SMEM = pl.BlockSpec(memory_space=pltpu.SMEM)
HBM = pl.BlockSpec(memory_space=pltpu.HBM)


def split_bf16(array):
    high = array.astype(np.float32).astype(BF16)
    low = (array - high.astype(np.float64)).astype(np.float32).astype(BF16)
    return high, low


def coarse_table(pad_rows):
    row = np.arange(pad_rows)
    step = (2 * row[None, :] + np.arange(2)[:, None]).reshape(-1)
    m0 = np.arange(LANES)
    angle = 2 * np.pi * ((step[None, :] * m0[:, None]) % COARSE) / COARSE
    used = (m0 < COARSE)[:, None]
    high, low = split_bf16(np.concatenate([np.cos(angle) * used, -np.sin(angle) * used], 0))
    return np.concatenate([high, low, high], 1)


def twiddle_table(lon_count, pix_dev):
    l = np.arange(LANES)
    m0 = np.arange(LANES)
    table = np.zeros((lon_count, 2, LANES, LANES), np.float32)
    for j in range(lon_count):
        first = j * pix_dev - RIM
        angle = 2 * np.pi * (((l[None, :] + first) * m0[:, None]) % NPHI) / NPHI
        table[j, 0] = np.cos(angle) * NPHI**-0.5
        table[j, 1] = -np.sin(angle) * NPHI**-0.5
    return table


def fine_table(num_sims):
    l = np.arange(LANES)
    table = np.zeros((2, HALF, num_sims, 2, num_sims, 2, LANES))
    for side in range(2):
        for d in range(HALF):
            m1 = d if side == 0 else TURNS - 1 - d
            angle = 2 * np.pi * ((l * m1) % LANES) / LANES
            for s in range(num_sims):
                table[side, d, s, 0, s, 0] = np.cos(angle)
                table[side, d, s, 0, s, 1] = np.sin(angle)
                table[side, d, s, 1, s, 0] = -np.sin(angle)
                table[side, d, s, 1, s, 1] = np.cos(angle)
    return split_bf16(table.reshape(4 * HALF * num_sims, 2 * num_sims * LANES))[0]


def analyse_kernel(
    live_ref, value_ref, weight_ref, cycle_ref, pixel_ref, coarse_hbm, twiddle_hbm, fine_hbm,
    out_ref, amount, index, left, right, coarse_ref, twiddle_ref, fine_ref, sems, *, pad_rows,
):
    tables = [
        pltpu.make_async_copy(coarse_hbm, coarse_ref, sems.at[0]),
        pltpu.make_async_copy(twiddle_hbm.at[lax.axis_index("lon")], twiddle_ref, sems.at[1]),
        pltpu.make_async_copy(fine_hbm, fine_ref, sems.at[2]),
    ]
    for copy in tables:
        copy.start()
    num_sims, rows = value_ref.shape[1:3]
    maps = num_sims * EXT_CYCLES
    alive = lax.broadcasted_iota(jnp.int32, (rows, LANES), 0) < live_ref[0]
    cycle = cycle_ref[...]
    for dp in range(2):
        pixel = pixel_ref[...] + dp
        index[dp] = (pixel >> 8).astype(F32)
        for s in range(num_sims):
            value = jnp.where(alive, value_ref[0, s], 0.0)
            here = value * weight_ref[dp]
            above = value * weight_ref[2 + dp]
            for c in range(EXT_CYCLES):
                amount[s * EXT_CYCLES + c, dp] = jnp.where(
                    cycle == c, here, jnp.where(cycle == c - 1, above, 0.0)
                )
    row_at = lax.broadcasted_iota(jnp.int32, (pad_rows, LANES), 0).astype(F32).astype(BF16)
    fine_at = [
        ((lax.broadcasted_iota(jnp.int32, (LANES, FINE), 1) - dp) & (FINE - 1)).astype(F32).astype(BF16)
        for dp in range(2)
    ]
    fine = (pixel_ref[...] & (FINE - 1)).astype(F32).T
    one, zero = jnp.ones((), BF16), jnp.zeros((), BF16)

    def all_rows(row):
        row = jnp.broadcast_to(row, (16, LANES)).astype(BF16)
        return jnp.concatenate([row] * (pad_rows // 16), 0)

    for k in range(rows):
        column = jnp.broadcast_to(fine[:, k : k + 1], (LANES, LANES)).astype(BF16)
        column = jnp.concatenate([column] * (FINE // LANES), 1)
        for dp in range(2):
            here = slice(FINE * k + LANES * dp, FINE * k + LANES * (dp + 1))
            hit = row_at == all_rows(index[dp, k : k + 1, :])
            for n in range(maps):
                left[n * pad_rows : (n + 1) * pad_rows, here] = jnp.where(
                    hit, all_rows(amount[n, dp, k : k + 1, :]), zero
                )
            right[here, :] = jnp.where(fine_at[dp] == column, one, zero)
    canvas = jnp.dot(left[...], right[...], preferred_element_type=F32)
    canvas = jnp.concatenate(
        [
            jnp.concatenate(
                [
                    canvas[n * pad_rows : (n + 1) * pad_rows, b * LANES : (b + 1) * LANES]
                    for n in range(maps)
                ],
                1,
            )
            for b in range(2)
        ],
        0,
    )
    high = canvas.astype(BF16)
    low = (canvas - high.astype(F32)).astype(BF16)
    for copy in tables:
        copy.wait()
    coarse = jnp.dot(
        coarse_ref[...], jnp.concatenate([high, high, low], 0), preferred_element_type=F32
    )
    turn_re, turn_im = twiddle_ref[0], twiddle_ref[1]
    blocks = []
    for c in range(EXT_CYCLES):
        lanes = []
        for s in range(num_sims):
            n = s * EXT_CYCLES + c
            real = coarse[:LANES, n * LANES : (n + 1) * LANES]
            imag = coarse[LANES:, n * LANES : (n + 1) * LANES]
            lanes += [real * turn_re - imag * turn_im, real * turn_im + imag * turn_re]
        blocks.append(jnp.concatenate(lanes, 1))
    turned = jnp.concatenate(blocks, 0).astype(BF16)
    dims = (((1,), (1,)), ((), ()))
    modes = lax.dot_general(fine_ref[...], turned, dims, preferred_element_type=F32)
    half = modes.shape[0] // 2
    modes = jnp.concatenate([modes[:half], modes[half:]], 1).astype(BF16)
    out_ref[...] = modes.reshape(out_ref.shape)


def analyse(live_rows, values, weights, cycle, pixel, pix_dev, lon_count):
    num_sims, rows = values.shape[1:3]
    pad_rows = -(-(pix_dev + 2 * RIM) // FINE // 16) * 16
    maps = num_sims * EXT_CYCLES
    coarse, fine = coarse_table(pad_rows), fine_table(num_sims)
    twiddle = twiddle_table(lon_count, pix_dev)
    out_shape = (HALF, 2 * num_sims, 2 * EXT_CYCLES * LANES)

    def whole(shape):
        return pl.BlockSpec(shape, lambda i: (0,) * len(shape))

    return pl.pallas_call(
        functools.partial(analyse_kernel, pad_rows=pad_rows),
        grid=(1,),
        in_specs=[
            SMEM,
            whole(values.shape),
            whole(weights.shape),
            whole(cycle.shape),
            whole(pixel.shape),
            HBM,
            HBM,
            HBM,
        ],
        out_specs=whole(out_shape),
        scratch_shapes=[
            pltpu.VMEM((maps, 2, rows, LANES), F32),
            pltpu.VMEM((2, rows, LANES), F32),
            pltpu.VMEM((maps * pad_rows, rows * FINE), BF16),
            pltpu.VMEM((rows * FINE, FINE), BF16),
            pltpu.VMEM(coarse.shape, BF16),
            pltpu.VMEM(twiddle.shape[1:], F32),
            pltpu.VMEM(fine.shape, BF16),
            pltpu.SemaphoreType.DMA((3,)),
        ],
        out_shape=jax.ShapeDtypeStruct(out_shape, BF16),
        compiler_params=pltpu.CompilerParams(vmem_limit_bytes=56 << 20),
    )(
        live_rows, values, weights, cycle, pixel,
        jnp.asarray(coarse), jnp.asarray(twiddle), jnp.asarray(fine),
    )


def first_pair_here(per_pair):
    place = lax.axis_index("band") * lax.axis_size("lon") + lax.axis_index("lon")
    return (place * lax.axis_size("pol") + lax.axis_index("pol")) * per_pair


def spread_kernel(filters_ref, out_ref):
    groups, _, group, wide = out_ref.shape
    first_pair = first_pair_here(groups * group)
    at = lax.broadcasted_iota(jnp.int32, (8, wide), 1)
    row = lax.broadcasted_iota(jnp.int32, (8, wide), 0)
    for f in range(2):
        full = jnp.concatenate([filters_ref[f : f + 1, :], jnp.zeros((1, wide - M), F32)], 1)
        full = jnp.broadcast_to(full, (8, wide))
        behind = pltpu.roll(full, 1, 1)
        ahead = full
        for bit in (1, 2, 4):
            ahead = jnp.where(row & bit != 0, pltpu.roll(ahead, wide - bit, 1), ahead)
        ahead = pltpu.roll(ahead, wide - first_pair, 1)
        for g in range(groups):
            for a in range(0, group, 8):
                first = g * group + a
                here = pltpu.roll(ahead, wide - first, 1) if first else ahead
                here = jnp.where(at < M - first_pair - first - row, here, behind)
                count = min(8, group - a)
                out_ref[g, f, a : a + count, :] = here[:count]


def spread_filters(filters, per_pair, cycles):
    group = grouping(per_pair, cycles)[0]
    wide = -(-(M + 1) // LANES) * LANES
    return pl.pallas_call(
        spread_kernel,
        in_specs=[VMEM],
        out_specs=VMEM,
        out_shape=jax.ShapeDtypeStruct((per_pair // group, 2, group, wide), F32),
        compiler_params=pltpu.CompilerParams(vmem_limit_bytes=8 << 20),
        cost_estimate=pl.CostEstimate(
            flops=20 * per_pair * wide, bytes_accessed=8 * per_pair * wide, transcendentals=0
        ),
    )(filters)


def grouping(per_pair, cycles):
    group = 2
    while per_pair % (2 * group) == 0 and 2 * group * cycles <= LANES:
        group *= 2
    return group, -(-group * cycles // LANES) * LANES


def swap_parts(array):
    even = lax.broadcasted_iota(jnp.int32, array.shape, 0) % 2 == 0
    return jnp.where(even, pltpu.roll(array, 7, 0), pltpu.roll(array, 1, 0))


def contract_kernel(
    modes_ref, spread_ref, w_hbm, x_hbm, out_ref,
    modes, factors, held, w_ref, x_ref, sems, *, direct,
):
    per_pair, cycles, row_width = w_ref.shape
    group, pad_depth = grouping(per_pair, cycles)
    groups, depth, half = per_pair // group, group * cycles, 4 * group
    edges = [*range(0, row_width - FINE, PIECE), row_width]
    tables = {}
    for g in range(groups):
        cuts = edges if g == 0 else [0, row_width]
        for n, (first, last) in enumerate(zip(cuts, cuts[1:])):
            part = (pl.ds(g * group, group), slice(None), pl.ds(first, last - first))
            tables[g, first] = [
                pltpu.make_async_copy(w_hbm.at[part], w_ref.at[part], sems.at[g, 2 * n]),
                pltpu.make_async_copy(x_hbm.at[part], x_ref.at[part], sems.at[g, 2 * n + 1]),
            ]
            for copy in tables[g, first]:
                copy.start()
    for comp in range(2):
        for side in range(2):
            for r in range(cycles):
                if direct:
                    total = jnp.zeros((4, LANES), F32)
                    lons = modes_ref.shape[0] // (2 * cycles)
                    for c in range(EXT_CYCLES):
                        band = r + 1 - c
                        if 0 <= band < cycles:
                            for j in range(lons):
                                lane = (side * EXT_CYCLES + c) * LANES
                                total += modes_ref[
                                    (band * lons + j) * 2 + comp, :, lane : lane + LANES
                                ].astype(F32)
                    total = total.astype(BF16).astype(F32)
                    total = jnp.concatenate([total, total], 0)
                else:
                    total = modes_ref[comp, side, r]
                modes[comp, side, r] = total

    lane = lax.broadcasted_iota(jnp.int32, (8, LANES), 1)
    sign = jnp.where(lax.broadcasted_iota(jnp.int32, (8, pad_depth), 0) % 2 == 0, 1.0, -1.0)
    own = (
        lax.broadcasted_iota(jnp.int32, (half, pad_depth), 0) // 4
        == lax.broadcasted_iota(jnp.int32, (half, pad_depth), 1) // cycles
    )
    copies = []
    for g in range(groups):
        for side in range(2):
            spread = []
            for comp in range(2):
                parts = []
                for first in range(0, pad_depth, LANES):
                    at = jnp.minimum(g * group + (first + lane) // cycles, per_pair - 1)
                    if direct and side == 1:
                        at = per_pair - 1 - at
                    value = jnp.zeros((8, LANES), F32)
                    for r in range(cycles):
                        taken = jnp.take_along_axis(
                            modes[comp, side, r], at, axis=1, mode="promise_in_bounds"
                        )
                        value = jnp.where((first + lane) % cycles == r, taken, value)
                    parts.append(value)
                spread.append(jnp.concatenate(parts, 1) if len(parts) > 1 else parts[0])
            q, u = spread
            pairs = ((-q, sign * swap_parts(u)), (-u, -sign * swap_parts(q)))
            for f, bases in enumerate(pairs):
                for n, base in enumerate(bases):
                    full = jnp.where(own, jnp.tile(base, (half // 8, 1)), 0.0).astype(BF16)
                    factors[
                        g, side, f * half : (f + 1) * half, n * pad_depth : (n + 1) * pad_depth
                    ] = full

    for g in range(groups):
        first_pair = first_pair_here(per_pair) + g * group
        def table_rows(cols):
            rows = []
            for ref in (w_ref, x_ref):
                rows.append(ref[g * group : (g + 1) * group, :, cols].reshape(depth, -1))
                if depth < pad_depth:
                    rows.append(jnp.zeros((pad_depth - depth, rows[0].shape[1]), BF16))
            return jnp.concatenate(rows, 0)

        def filtered(rows, side, cols):
            both = jnp.dot(factors[g, side], rows, preferred_element_type=F32)
            width = both.shape[1]
            total = []
            for a in range(half // 8):
                pair = 2 * a
                e, b = (
                    jnp.concatenate(
                        [
                            jnp.broadcast_to(spread_ref[g, f, pair + n : pair + n + 1, cols], (4, width))
                            for n in range(2)
                        ],
                        0,
                    )
                    for f in range(2)
                )
                total.append(e * both[8 * a : 8 * a + 8] + b * both[half + 8 * a : half + 8 * a + 8])
            return jnp.concatenate(total, 0)

        def put(total, slot, cols):
            held[slot, :, :, :, cols] = total.astype(BF16).reshape(group, 2, 2, -1)

        def send(first, last):
            piece = pl.ds(first, last - first)
            copy = pltpu.make_async_copy(
                held.at[g, :, :, :, piece],
                out_ref.at[pl.ds(g * group, group), :, :, piece],
                sems.at[g, 2 * len(edges) + first // PIECE],
            )
            copy.start()
            copies.append(copy)

        mixed = pl.multiple_of((M - 1 - first_pair) // FINE * FINE, FINE)

        def put_mixed():
            cols = pl.ds(mixed, FINE)
            rows = table_rows(cols)
            pair = first_pair + lax.broadcasted_iota(jnp.int32, (half, FINE), 0) // 4
            at = mixed + lax.broadcasted_iota(jnp.int32, (half, FINE), 1)
            near, far = (filtered(rows, side, cols) for side in range(2))
            put(jnp.where(at < M - pair, near, far), g, cols)

        if g > 0:
            for copy in tables[g, 0]:
                copy.wait()
            put_mixed()
        for start in range(0, row_width, FINE):
            if g == 0 and (g, start) in tables:
                for copy in tables[g, start]:
                    copy.wait()
            stop = min(start + FINE, row_width)
            cols = slice(start, stop)
            side = (start >= M - first_pair).astype(jnp.int32)
            slot = g if g == 0 else jnp.where(start == mixed, groups, g)
            put(filtered(table_rows(cols), side, cols), slot, cols)
            if g > 0 and stop in edges:
                send(edges[edges.index(stop) - 1], stop)
        if g == 0:
            put_mixed()
            for first, last in zip(edges, edges[1:]):
                send(first, last)
    for copy in copies:
        copy.wait()


def contract(modes, spread, table_w, table_x, direct):
    per_pair, cycles, row_width = table_w.shape
    group, pad_depth = grouping(per_pair, cycles)
    groups = per_pair // group
    return pl.pallas_call(
        functools.partial(contract_kernel, direct=direct),
        in_specs=[VMEM, VMEM, HBM, HBM],
        out_specs=HBM,
        out_shape=jax.ShapeDtypeStruct((per_pair, 2, 2, row_width), BF16),
        scratch_shapes=[
            pltpu.VMEM((2, 2, cycles, 8, LANES), F32),
            pltpu.VMEM((groups, 2, 8 * group, 2 * pad_depth), BF16),
            pltpu.VMEM((groups + 1, group, 2, 2, row_width), BF16),
            pltpu.VMEM(table_w.shape, BF16),
            pltpu.VMEM(table_x.shape, BF16),
            pltpu.SemaphoreType.DMA((groups, 2 * 4 + 4)),
        ],
        compiler_params=pltpu.CompilerParams(vmem_limit_bytes=50 << 20),
    )(modes, spread, table_w, table_x)


def by_owner(payload, per_pair):
    split = COARSE // per_pair
    parts = payload.reshape(HALF, 4, 2, EXT_CYCLES, LANES)[..., :COARSE]
    parts = jnp.stack([parts[:, :, 0], parts[:, :, 1, :, ::-1]], 2)
    parts = parts.reshape(HALF, 4, 2, EXT_CYCLES, split, per_pair)
    parts = jnp.transpose(parts, (0, 4, 1, 2, 3, 5))
    return parts.reshape(HALF * split, 4, 2, EXT_CYCLES, per_pair)


def sum_sources(received, bands, lons):
    per_pair = received.shape[-1]
    parts = received.astype(F32).reshape(bands, lons, 2, 4, 2, EXT_CYCLES, per_pair).sum(1)
    parts = jnp.pad(parts, ((1, 1), (0, 0), (0, 0), (0, 0), (0, 0), (0, 0)))
    total = sum(parts[2 - c : 2 - c + bands, :, :, :, c] for c in range(EXT_CYCLES))
    total = jnp.transpose(total, (1, 3, 0, 2, 4)).astype(BF16).astype(F32)
    total = jnp.concatenate([total, total], 3)
    return jnp.pad(total, ((0, 0),) * 4 + ((0, LANES - per_pair),))


def body(
    residual_cot, splat_weights, sample_cycle, sample_pixel, live_rows, table_w, table_x, filters
):
    bands = lax.axis_size("band")
    lons = lax.axis_size("lon")
    owners = ("band", "lon", "pol")
    per_pair = table_w.shape[0]
    payload = analyse(
        live_rows, residual_cot, splat_weights, sample_cycle, sample_pixel, NPHI // lons, lons
    )
    direct = per_pair == COARSE
    if not direct:
        payload = by_owner(payload, per_pair)
    modes = lax.all_to_all(payload, owners, 0, 0, tiled=True)
    if not direct:
        modes = sum_sources(modes, bands, lons)
    spread = spread_filters(filters, per_pair, table_w.shape[1])
    return contract(modes, spread, table_w, table_x, direct)


def solution(mesh):
    in_specs = (
        P("pol", "sky", "band", "lon"),
        P("sky", "band", "lon"),
        P(("sky", "band"), "lon"),
        P(("sky", "band"), "lon"),
        P(("sky", "band", "lon")),
        P(("band", "lon", "pol"), None, None),
        P(("band", "lon", "pol"), None, None),
        P(),
    )
    out_specs = P(("band", "lon", "pol"), "sky", None, None)
    return jax.shard_map(body, mesh=mesh, in_specs=in_specs, out_specs=out_specs, check_vma=False)
```
